512 devices in a mesh: gx: 32 (over x_lo, z), gy: 16 (over y, x_hi, core).
Axes of the slice: x: 4 (x_hi: 2, x_lo: 2; x = x_hi * 2 + x_lo), y: 4, z: 16, core: 2. Of those that a mesh axis runs over, the one named last changes fastest.
Arguments:
- velocity: float32 [3, 1, 4096, 10240], P(None, None, 'gy', 'gx'), may hold values from -12 to 12
- grid_x: float32 [33], replicated, may hold values from 0.05 to 1
- grid_y: float32 [4096, 33], P('gy'), may hold values from 0.05 to 1
- test_x: float32 [33], replicated, may hold values from 0.05 to 1
- test_y: float32 [4096, 33], P('gy'), may hold values from 0.05 to 1
Outputs:
- subgrid: float32 [6, 1, 4096, 10240], P(None, None, 'gy', 'gx')
- germano: float32 [6, 1, 4096, 10240], P(None, None, 'gy', 'gx')
The draws below stay inside these ranges and needn't reach their ends.
All inputs are finite; a program needn't handle non-finite values.
Results may differ from the reference program's by a relative error of at most 0.0001.
Values sent between devices are 32-bit elements; how exact they have to be, the bound alone decides.
No kernel may reach another device: no remote copies, remote signals or barrier semaphores. Data moves between devices by JAX's collectives and lax.ppermute only.
A program may use at most 64 MiB of HBM per device.

```python
import math
import jax
import jax.numpy as jnp
from jax import lax

NZ = 1
TAPS = 33
NX = 10240
NY = 4096


def block_scale(key, dims, cuts, low, top_value):
    gain, own = 1.0, jax.random.fold_in(key, 6)
    for position, shards_of in cuts:
        draws = jnp.exp(jax.random.uniform(jax.random.fold_in(own, position), (shards_of,), jnp.float32, low / len(cuts), top_value / len(cuts)))
        gain = gain * jnp.repeat(draws, dims[position] // shards_of).reshape([-1 if axis == position else 1 for axis in range(len(dims))])
    return gain


def scatter_about(rng, extent, deviation, most, pieces=(), kind=jnp.bfloat16):
    level = block_scale(rng, extent, pieces, -0.22, 0.18) if pieces else 1.0
    values = jax.random.normal(rng, extent, jnp.float32) * deviation * level
    return jnp.minimum(jnp.maximum(values, -most), most).astype(kind)


def setup_inputs(seed: int = 0) -> dict:
    keys = jax.random.split(jax.random.key(seed), 6)
    return {
        "velocity": scatter_about(keys[0], (3, NZ, NY, NX), 2.0, 12.0, ((2, 16), (3, 32)), jnp.float32),
        "grid_x": jnp.clip(jnp.exp(jax.random.uniform(keys[1], (TAPS,), jnp.float32, math.log(0.05), math.log(1.0))), 0.05, 1.0),
        "grid_y": jnp.clip(jnp.exp(math.log(1.0) - 2.9957323 * jax.random.uniform(keys[2], (NY, TAPS), jnp.float32) ** block_scale(keys[2], (NY, TAPS), ((0, 16),), -0.2, 0.2)), 0.05, 1.0),
        "test_x": jnp.clip(jnp.exp(jax.random.uniform(keys[3], (TAPS,), jnp.float32, math.log(0.05), math.log(1.0))), 0.05, 1.0),
        "test_y": jnp.clip(jnp.exp(math.log(1.0) - 2.9957323 * jax.random.uniform(keys[4], (NY, TAPS), jnp.float32) ** block_scale(keys[4], (NY, TAPS), ((0, 16),), -0.2, 0.2)), 0.05, 1.0),
    }


COMPONENT_PAIRS = [(0, 0), (0, 1), (0, 2), (1, 1), (1, 2), (2, 2)]


def x_smooth(field, weights):
    taps_count = weights.shape[0]
    margin = (taps_count - 1) // 2
    normed = weights / jnp.sum(weights)
    padded = jnp.concatenate([field[..., -margin:], field, field[..., :margin]], axis=-1)
    lead_shape = field.shape[:-1]
    flat = padded.reshape((-1, 1, padded.shape[-1]))
    kernel = normed.reshape((1, 1, taps_count)).astype(field.dtype)
    result = lax.conv_general_dilated(flat, kernel, (1,), "VALID", precision=lax.Precision.HIGHEST)
    return result.reshape(lead_shape + (field.shape[-1],))


def y_smooth(field, table):
    rows_count = table.shape[0]
    taps_count = table.shape[1]
    margin = (taps_count - 1) // 2
    global_row = jnp.arange(rows_count, dtype=jnp.int32)
    source = global_row[:, None] + jnp.arange(taps_count, dtype=jnp.int32)[None, :] - margin
    inside = (source >= 0) & (source < rows_count)
    masked = jnp.where(inside, table, jnp.zeros_like(table))
    normed = masked / jnp.sum(masked, axis=1, keepdims=True)
    padded = jnp.pad(field, ((0, 0), (margin, margin), (0, 0)))
    result = jnp.zeros_like(field)
    for offset in range(taps_count):
        result = result + normed[:, offset][None, :, None] * padded[:, offset:offset + rows_count, :]
    return result


def smooth(field, weights, table):
    return y_smooth(x_smooth(field, weights), table)


def reference(velocity, grid_x, grid_y, test_x, test_y):
    coarse = [smooth(velocity[comp], grid_x, grid_y) for comp in range(3)]
    tested = [smooth(coarse[comp], test_x, test_y) for comp in range(3)]
    subgrid = []
    germano = []
    for first_comp, second_comp in COMPONENT_PAIRS:
        product = velocity[first_comp] * velocity[second_comp]
        subgrid.append(smooth(product, grid_x, grid_y) - coarse[first_comp] * coarse[second_comp])
        resolved = coarse[first_comp] * coarse[second_comp]
        germano.append(smooth(resolved, test_x, test_y) - tested[first_comp] * tested[second_comp])
    return jnp.stack(subgrid), jnp.stack(germano)
```

```python
import jax
import jax.numpy as jnp
from jax import lax
from jax.experimental import pallas as pl
from jax.experimental.pallas import tpu as pltpu
from jax.sharding import PartitionSpec as P

BF = jnp.bfloat16
F32 = jnp.float32
HALF = 16
TAPS = 33
HALO = 32
NX = 320
NY = 256
RING = 384
NX_READ = NX + 2 * HALO
NX_COARSE = NX + 2 * HALF
QUARTER = NX_READ // 4
PAIRS = [(0, 0), (0, 1), (0, 2), (1, 1), (1, 2), (2, 2)]
VMEM = pl.BlockSpec(memory_space=pltpu.VMEM)
SMEM = pl.BlockSpec(memory_space=pltpu.SMEM)
ANY = pl.BlockSpec(memory_space=pl.ANY)


def split(x):
    hi = x.astype(BF)
    return hi, (x - hi.astype(F32)).astype(BF)


def read_kernel(v_ref, left_ref, right_ref, table_ref, read, to_low, to_high):
    for f in range(3):
        read[f, 0:HALO] = left_ref[f]
        read[f, HALO : HALO + NX] = v_ref[f]
        read[f, HALO + NX :] = right_ref[f]
        quarters = [pl.ds(QUARTER * q, QUARTER) for q in range(4)]
        to_low[f, 0:QUARTER] = jnp.concatenate([read[f, r, 0:HALO] for r in quarters], axis=1)
        to_high[f, 0:QUARTER] = jnp.concatenate([read[f, r, NY - HALO : NY] for r in quarters], axis=1)
    for f in range(3):
        to_low[f, QUARTER:] = jnp.zeros((HALF, 128), F32)
        to_high[f, QUARTER:] = jnp.zeros((HALF, 128), F32)
    to_low[0, QUARTER:, 0:TAPS] = table_ref[0:HALF, :]
    to_high[0, QUARTER:, 0:TAPS] = table_ref[NY - HALF : NY, :]


def make_read(velocity, left, right, table):
    edge = jax.ShapeDtypeStruct((3, QUARTER + HALF, 128), F32)
    return pl.pallas_call(
        read_kernel,
        out_shape=[jax.ShapeDtypeStruct((3, NX_READ, NY), F32), edge, edge],
        in_specs=[VMEM] * 4,
        out_specs=[VMEM] * 3,
        compiler_params=pltpu.CompilerParams(vmem_limit_bytes=16 << 20),
    )(velocity, left, right, table)


def norm_y(table, first_row, total_rows):
    row = first_row + lax.broadcasted_iota(jnp.int32, table.shape, 0)
    tap = lax.broadcasted_iota(jnp.int32, table.shape, 1)
    source = row + tap - HALF
    masked = jnp.where((source >= 0) & (source < total_rows) & (tap < TAPS), table, 0.0)
    total = jnp.sum(masked, axis=1, keepdims=True)
    inside = (row[:, :1] >= 0) & (row[:, :1] < total_rows)
    return masked / jnp.where(inside, total, 1.0)


def rolled(part, offset, lanes):
    m = part.shape[0]
    wide = jnp.concatenate([part, jnp.zeros((m, lanes - 128), F32)], axis=1)
    return pltpu.roll(wide, offset % lanes, 1, stride=1, stride_axis=0)


def y_matrix(weights, lane, out, row):
    m = weights.shape[0]
    high = weights.astype(BF).astype(F32)
    hi = rolled(high, lane - HALF, RING)
    lo = rolled(weights - high, lane - HALF, RING)
    edge = hi[:, NY:] + pltpu.roll(hi[:, NY:], 64, 1)
    parts = [hi[:, :NY], hi[:, :NY], lo[:, :NY], edge, lo[:, NY:]]
    out[row : row + m, :] = jnp.concatenate(parts, axis=1).astype(BF)


def lanes_of(hi, lo):
    lane = lax.broadcasted_iota(jnp.int32, (hi.shape[0], 128), 1)
    outer = (lane < HALO) | (lane >= 128 - HALO)
    low = pltpu.roll(lo[:, NY:].astype(F32), 64, 1).astype(BF)
    edge = jnp.where(outer, hi[:, NY:], low)
    return jnp.concatenate([hi[:, :NY], lo[:, :NY], hi[:, :NY], edge, hi[:, NY:]], axis=1)


def filter_y(x, matrix):
    return lax.dot_general(
        lanes_of(*split(x)), matrix, (((1,), (1,)), ((), ())), preferred_element_type=F32
    )


def x_taps(taps_ref, rows):
    lane = lax.broadcasted_iota(jnp.int32, (rows, 128), 1)
    taps = jnp.zeros((rows, 128), F32)
    for t in range(TAPS):
        taps = jnp.where(lane == t, taps_ref[t], taps)
    return taps / jnp.sum(taps, axis=1, keepdims=True)


def x_matrix(taps_ref, m):
    k = m + 2 * HALF
    lanes = -(-3 * k // 128) * 128
    taps = x_taps(taps_ref, m)
    high = taps.astype(BF).astype(F32)
    low = taps - high
    total = rolled(high, 0, lanes) + rolled(high, k, lanes) + rolled(low, 2 * k, lanes)
    return total.astype(BF)


def filter_x(matrix, x, start, m):
    k = m + 2 * HALF
    hi, lo = split(x[start : start + k])
    spare = matrix.shape[1] - 3 * k
    parts = [hi, lo, hi]
    if spare:
        parts.append(jnp.zeros((spare, x.shape[1]), BF))
    return jnp.dot(matrix, jnp.concatenate(parts, axis=0), preferred_element_type=F32)


def main_kernel(
    grid_x, test_x, center, low_ref, high_ref, grid_y, test_y, subgrid, germano,
    read, smooth, coarse, tested, y_grid, y_test, tab_g, tab_t, buf_s, buf_g, sems,
):
    first_row = lax.axis_index("gy") * NY
    total_rows = lax.axis_size("gy") * NY
    tab_g[...] = jnp.zeros_like(tab_g)
    tab_t[...] = jnp.zeros_like(tab_t)
    tab_g[0:HALF, 0:TAPS] = low_ref[0, QUARTER:, 0:TAPS]
    tab_g[HALF : HALF + NY, 0:TAPS] = grid_y[...]
    tab_g[HALF + NY :, 0:TAPS] = high_ref[0, QUARTER:, 0:TAPS]
    tab_t[:, 0:TAPS] = test_y[...]
    w_grid = norm_y(tab_g[...], first_row - HALF, total_rows)
    w_test = norm_y(tab_t[...], first_row, total_rows)
    for s in (0, 128):
        y_matrix(w_grid[HALF + s : HALF + s + 128], s, y_grid, s)
        y_matrix(w_test[s : s + 128], s, y_test, s)
    y_grid[NY:, :] = jnp.zeros((128, 4 * NY), BF)
    y_matrix(w_grid[HALF + NY :], NY, y_grid, NY)
    y_matrix(w_grid[0:HALF], RING - HALF, y_grid, RING - HALF)
    x_grid = {m: x_matrix(grid_x, m) for m in (128, 96, 64)}
    x_test = {m: x_matrix(test_x, m) for m in (128, 64)}
    copies = []

    def send(buffer, out, p, sem):
        copy = pltpu.make_async_copy(buffer.at[p], out.at[p], sem)
        copy.start()
        copies.append(copy)

    for f in range(3):
        read[f, :, 0:NY] = center[f]
        for q in range(4):
            lanes = slice(HALO * q, HALO * (q + 1))
            read[f, QUARTER * q : QUARTER * (q + 1), NY:] = jnp.concatenate(
                [high_ref[f, 0:QUARTER, lanes], jnp.zeros((QUARTER, 64), F32), low_ref[f, 0:QUARTER, lanes]], axis=1
            )
    for f in range(3):
        for start, m in ((0, 128), (128, 128), (256, 96)):
            smooth[f, start : start + m] = filter_x(x_grid[m], read[f], start, m)
        coarse[f] = filter_y(smooth[f], y_grid[...])
    for p, (i, j) in enumerate(PAIRS):
        product = read[i, HALF : HALF + NX_COARSE] * read[j, HALF : HALF + NX_COARSE]
        for start, m in ((0, 128), (128, 128), (256, 64)):
            smooth[3 + p, start : start + m] = filter_x(x_grid[m], product, start, m)
        own = slice(HALF, HALF + NX)
        stress = filter_y(smooth[3 + p, 0:NX], y_grid[0:NY, :])
        buf_s[p] = stress - coarse[i, own, 0:NY] * coarse[j, own, 0:NY]
        send(buf_s, subgrid, p, sems.at[p])
    for f in range(9):
        field = coarse[f] if f < 3 else coarse[PAIRS[f - 3][0]] * coarse[PAIRS[f - 3][1]]
        for start, m in ((0, 128), (128, 128), (256, 64)):
            smooth[f, start : start + m] = filter_x(x_test[m], field, start, m)
        result = filter_y(smooth[f, 0:NX], y_test[...])
        if f < 3:
            tested[f] = result
        else:
            i, j = PAIRS[f - 3]
            buf_g[f - 3] = result - tested[i] * tested[j]
            send(buf_g, germano, f - 3, sems.at[3 + f])
    for copy in copies:
        copy.wait()


def main(grid_x, test_x, center, low, high, grid_y, test_y):
    out = jax.ShapeDtypeStruct((6, NX, NY), F32)
    return pl.pallas_call(
        main_kernel,
        out_shape=[out, out],
        in_specs=[SMEM, SMEM] + [VMEM] * 5,
        out_specs=[ANY, ANY],
        scratch_shapes=[
            pltpu.VMEM((3, NX_READ, RING), F32),
            pltpu.VMEM((9, NX_COARSE, RING), F32),
            pltpu.VMEM((3, NX_COARSE, RING), F32),
            pltpu.VMEM((3, NX, NY), F32),
            pltpu.VMEM((RING, 4 * NY), BF),
            pltpu.VMEM((NY, 4 * NY), BF),
            pltpu.VMEM((NY + 2 * HALF, 128), F32),
            pltpu.VMEM((NY, 128), F32),
            pltpu.VMEM((6, NX, NY), F32),
            pltpu.VMEM((6, NX, NY), F32),
            pltpu.SemaphoreType.DMA((12,)),
        ],
        compiler_params=pltpu.CompilerParams(vmem_limit_bytes=40 << 20),
    )(grid_x, test_x, center, low, high, grid_y, test_y)


def shifts(axis, periodic):
    count = lax.axis_size(axis)
    up = [(i, i + 1) for i in range(count - 1)]
    if periodic:
        up.append((count - 1, 0))
    return up, [(b, a) for a, b in up]


def local(velocity, grid_x, grid_y, test_x, test_y):
    velocity = velocity.reshape(3, NY, NX).swapaxes(1, 2)
    up, down = shifts("gx", True)
    left = lax.ppermute(velocity[:, NX - HALO :], "gx", up)
    right = lax.ppermute(velocity[:, :HALO], "gx", down)
    center, to_low, to_high = make_read(velocity, left, right, grid_y)
    up, down = shifts("gy", False)
    low = lax.ppermute(to_high, "gy", up)
    high = lax.ppermute(to_low, "gy", down)
    outs = main(grid_x, test_x, center, low, high, grid_y, test_y)
    return tuple(out.swapaxes(1, 2).reshape(6, 1, NY, NX) for out in outs)


def solution(mesh):
    placed = (P(None, None, "gy", "gx"), P(), P("gy", None), P(), P("gy", None))
    return jax.shard_map(
        local,
        mesh=mesh,
        in_specs=placed,
        out_specs=(P(None, None, "gy", "gx"), P(None, None, "gy", "gx")),
        check_vma=False,
    )
```

```python
import jax
import jax.numpy as jnp
from jax import lax
from jax.experimental import pallas as pl
from jax.experimental.pallas import tpu as pltpu
from jax.sharding import PartitionSpec as P

BF = jnp.bfloat16
F32 = jnp.float32
HALF = 16
TAPS = 33
HALO = 32
NX = 320
NY = 256
RING = 384
NX_READ = NX + 2 * HALO
NX_COARSE = NX + 2 * HALF
TAP_ROWS = 40
QUARTER = NX_READ // 4
PAIRS = [(0, 0), (0, 1), (0, 2), (1, 1), (1, 2), (2, 2)]
VMEM = pl.BlockSpec(memory_space=pltpu.VMEM)
SMEM = pl.BlockSpec(memory_space=pltpu.SMEM)
HBM = pl.BlockSpec(memory_space=pltpu.HBM)


def cost(us):
    return pl.CostEstimate(flops=us * 10**9, bytes_accessed=10**6, transcendentals=0)


def split(x):
    hi = x.astype(BF)
    return hi, (x - hi.astype(F32)).astype(BF)


def is_even(axis):
    return lax.rem(lax.axis_index(axis), 2) == 0


def edges(velocity):
    even = is_even("gx")
    low, high = velocity[:, :HALO], velocity[:, NX - HALO :]
    return jnp.where(even, low, high), jnp.where(even, high, low)


def pack_kernel(own, x_first, x_second, taps, first, second, read, table):
    even_x, even_y = is_even("gx"), is_even("gy")
    for f in range(3):
        read[f, HALO : HALO + NX] = own[f]
        read[f, 0:HALO] = jnp.where(even_x, x_first[f], x_second[f])
        read[f, HALO + NX :] = jnp.where(even_x, x_second[f], x_first[f])
        quarters = [pl.ds(QUARTER * q, QUARTER) for q in range(4)]
        low = jnp.concatenate([read[f, r, 0:HALO] for r in quarters], axis=1)
        high = jnp.concatenate([read[f, r, NY - HALO : NY] for r in quarters], axis=1)
        first[QUARTER * f : QUARTER * (f + 1), :] = jnp.where(even_y, low, high)
        second[QUARTER * f : QUARTER * (f + 1), :] = jnp.where(even_y, high, low)
    table[...] = jnp.zeros_like(table)
    table[0:TAPS, :] = taps[...]
    groups = [pl.ds(8 * g, 8) for g in range(TAP_ROWS // 8)]
    spare = jnp.zeros((8, 128 - 2 * TAP_ROWS), F32)
    low = jnp.concatenate([table[r, 0:HALF] for r in groups] + [spare], axis=1)
    high = jnp.concatenate([table[r, NY - HALF : NY] for r in groups] + [spare], axis=1)
    first[3 * QUARTER :, :] = jnp.where(even_y, low, high)
    second[3 * QUARTER :, :] = jnp.where(even_y, high, low)


def pack(own, x_first, x_second, taps):
    edge = jax.ShapeDtypeStruct((3 * QUARTER + 8, 128), F32)
    return pl.pallas_call(
        pack_kernel,
        out_shape=[edge, edge, jax.ShapeDtypeStruct((3, NX_READ, NY), F32)],
        in_specs=[VMEM] * 4,
        out_specs=[VMEM] * 3,
        scratch_shapes=[pltpu.VMEM((TAP_ROWS, NY), F32)],
        compiler_params=pltpu.CompilerParams(vmem_limit_bytes=8 << 20),
        cost_estimate=cost(5),
    )(own, x_first, x_second, taps)


def norm_y(taps, cell, total_cells):
    tap = lax.broadcasted_iota(jnp.int32, taps.shape, 0)
    source = cell + tap - HALF
    masked = jnp.where((source >= 0) & (source < total_cells) & (tap < TAPS), taps, 0.0)
    total = jnp.sum(masked, axis=0, keepdims=True)
    weights = masked / jnp.where(total > 0, total, 1.0)
    high = weights.astype(BF).astype(F32)
    return high, weights - high


def slanted(part, rows, cells):
    x = jnp.concatenate([part, jnp.zeros((rows - part.shape[0], 128), F32)], axis=0)
    lane = lax.broadcasted_iota(jnp.int32, x.shape, 1)
    step = 1
    while step < cells:
        x = jnp.where((lane & step) != 0, pltpu.roll(x, step, 0), x)
        step *= 2
    return x


def rolled(part, offset, lanes):
    m = part.shape[0]
    wide = jnp.concatenate([part, jnp.zeros((m, lanes - 128), F32)], axis=1)
    return pltpu.roll(wide, offset % lanes, 1, stride=1, stride_axis=0)


def y_matrix(taps_ref, first_cell, total_cells, table, out):
    table[...] = jnp.zeros_like(table)
    table[0:TAPS, :] = taps_ref[...]
    out[...] = jnp.zeros_like(out)
    for s in (0, 128):
        cell = first_cell + s + lax.broadcasted_iota(jnp.int32, (TAP_ROWS, 128), 1)
        weights = norm_y(table[:, s : s + 128], cell, total_cells)
        hi, lo = (slanted(part, 128 + 2 * HALF, 128).astype(BF) for part in weights)
        own = slice(HALF, 128 + 2 * HALF) if s == 0 else slice(0, 128 + HALF)
        halo = slice(0, HALF) if s == 0 else slice(128 + HALF, 128 + 2 * HALF)
        row = 0 if s == 0 else 128 - HALF
        halo_row = 128 - HALF if s == 0 else 0
        lanes = slice(s, s + 128)
        for base, part in ((0, hi), (NY, hi), (2 * NY, lo)):
            out[base + row : base + row + 128 + HALF, lanes] = part[own]
        for base, part in ((halo_row, hi), ((halo_row + 64) % 128, hi), (128 + halo_row, lo)):
            out[3 * NY + base : 3 * NY + base + HALF, lanes] = part[halo]


def outer_matrix(higher, lower, first_cell, total_cells, out):
    lane = lax.broadcasted_iota(jnp.int32, (TAP_ROWS, 128), 1)
    groups = [slice(HALF * g, HALF * (g + 1)) for g in range(TAP_ROWS // 8)]
    spare = jnp.zeros((8, 128 - 2 * HALF), F32)
    taps = [jnp.concatenate([higher[:, g], spare, lower[:, g]], axis=1) for g in groups]
    cell = first_cell + jnp.where(lane < 64, NY + lane, lane - 128)
    weights = norm_y(jnp.concatenate(taps, axis=0), cell, total_cells)
    hi, lo = (slanted(part, 3 * HALF, HALF) for part in weights)
    low_side = lax.broadcasted_iota(jnp.int32, hi.shape, 1) >= 64
    out[...] = jnp.zeros_like(out)
    ends = []
    for part in (hi, lo):
        high_end = jnp.where(low_side, 0.0, part).astype(BF)
        low_end = jnp.where(low_side, part, 0.0).astype(BF)
        ends.append((high_end[HALF:], low_end[0:HALO], high_end[0:HALF], low_end[HALO:]))
    for base, part in ((0, 0), (64, 0), (128, 1)):
        out[base : base + HALO, :] = ends[part][0]
    for base, part in ((96, 0), (32, 0), (128 + 96, 1)):
        out[base : base + HALO, :] = ends[part][1]
    for base, part in ((112, 0), (16, 0), (48, 1)):
        out[256 + base : 256 + base + HALF, :] = ends[part][2]
    for base, part in ((0, 0), (32, 0), (64, 1)):
        out[256 + base : 256 + base + HALF, :] = ends[part][3]


def halo_lanes(hi, lo):
    lane = lax.broadcasted_iota(jnp.int32, hi.shape, 1)
    outer = (lane < HALO) | (lane >= 128 - HALO)
    return jnp.where(outer, hi, pltpu.roll(lo.astype(F32), 64, 1).astype(BF))


def lanes_of(hi, lo):
    own = [hi[:, :NY], lo[:, :NY], hi[:, :NY]]
    return jnp.concatenate(own + [halo_lanes(hi[:, NY:], lo[:, NY:]), hi[:, NY:]], axis=1)


def times(left, matrix):
    return jnp.dot(left, matrix, preferred_element_type=F32)


def x_taps(taps_ref, rows):
    lane = lax.broadcasted_iota(jnp.int32, (rows, 128), 1)
    taps = jnp.zeros((rows, 128), F32)
    for t in range(TAPS):
        taps = jnp.where(lane == t, taps_ref[t], taps)
    return taps / jnp.sum(taps, axis=1, keepdims=True)


def x_matrix(taps_ref, m):
    k = m + 2 * HALF
    lanes = -(-3 * k // 128) * 128
    taps = x_taps(taps_ref, m)
    high = taps.astype(BF).astype(F32)
    low = taps - high
    total = rolled(high, 0, lanes) + rolled(high, k, lanes) + rolled(low, 2 * k, lanes)
    return total.astype(BF)


def filter_x(matrix, x, start, m):
    k = m + 2 * HALF
    hi, lo = split(x[start : start + k])
    spare = matrix.shape[1] - 3 * k
    parts = [hi, lo, hi]
    if spare:
        parts.append(jnp.zeros((spare, x.shape[1]), BF))
    return jnp.dot(matrix[...], jnp.concatenate(parts, axis=0), preferred_element_type=F32)


def matrix_kernel(grid_x, test_x, grid_y, test_y, y_grid, y_test, *rest):
    first_cell = lax.axis_index("gy") * NY
    total_cells = lax.axis_size("gy") * NY
    table = rest[-1]
    for out, (taps, m) in zip(rest[:-1], X_PARTS):
        out[...] = x_matrix((grid_x, test_x)[taps], m)
    y_matrix(grid_y, first_cell, total_cells, table, y_grid)
    y_matrix(test_y, first_cell, total_cells, table, y_test)


X_PARTS = [(0, 128), (0, 96), (0, 64), (1, 128), (1, 64)]


def matrices(grid_x, test_x, grid_y, test_y):
    return pl.pallas_call(
        matrix_kernel,
        out_shape=[
            jax.ShapeDtypeStruct((4 * NY, NY), BF),
            jax.ShapeDtypeStruct((4 * NY, NY), BF),
        ]
        + [jax.ShapeDtypeStruct((m, -(-3 * (m + 2 * HALF) // 128) * 128), BF) for _, m in X_PARTS],
        in_specs=[SMEM, SMEM, VMEM, VMEM],
        out_specs=[VMEM] * (2 + len(X_PARTS)),
        scratch_shapes=[pltpu.VMEM((TAP_ROWS, NY), F32)],
        compiler_params=pltpu.CompilerParams(vmem_limit_bytes=8 << 20),
        cost_estimate=cost(2),
    )(grid_x, test_x, grid_y, test_y)


VELOCITY_TILES = ((0, 128), (128, 128), (256, 96))
INNER_TILES = ((0, 128), (128, 128), (256, 64))


STARTS = [NX_COARSE * f for f in range(3)] + [3 * NX_COARSE + NX * p for p in range(6)]
STACK = 3 * NX_COARSE + 6 * NX


def own_kernel(read, x128, x96, x64, y_grid, part, near, hi, lo):
    x_grid = {128: x128, 96: x96, 64: x64}
    for f in range(9):
        if f < 3:
            field, tiles = read[f], VELOCITY_TILES
        else:
            i, j = PAIRS[f - 3]
            inner = slice(HALF, HALF + NX_COARSE)
            field, tiles = read[i, inner] * read[j, inner], INNER_TILES
        for start, m in tiles:
            rows = slice(STARTS[f] + start, STARTS[f] + start + m)
            hi[rows], lo[rows] = split(filter_x(x_grid[m], field, start, m))
        rows = slice(STARTS[f], STARTS[f] + (NX_COARSE if f < 3 else NX))
        if f < 3:
            near[f] = near_lanes(hi[rows], lo[rows])
    part[...] = times(jnp.concatenate([hi[...], lo[...], hi[...]], axis=1), y_grid[0 : 3 * NY])


def near_lanes(hi, lo):
    lane = lax.broadcasted_iota(jnp.int32, (hi.shape[0], 128), 1)
    ends = [jnp.where(lane < HALF, x[:, 0:128], x[:, 128:NY]).astype(F32) for x in (hi, lo)]
    low, again = pltpu.roll(ends[1], 32, 1), pltpu.roll(ends[0], 64, 1)
    ends = jnp.where((lane < HALF) | (lane >= 128 - HALF), ends[0], jnp.where(lane < 48, low, again))
    return ends.astype(BF)


def filter_own(read, x_grid, y_grid):
    return pl.pallas_call(
        own_kernel,
        out_shape=[
            jax.ShapeDtypeStruct((STACK, NY), F32),
            jax.ShapeDtypeStruct((3, NX_COARSE, 128), BF),
        ],
        in_specs=[VMEM] * 5,
        out_specs=[VMEM] * 2,
        scratch_shapes=[pltpu.VMEM((STACK, NY), BF), pltpu.VMEM((STACK, NY), BF)],
        compiler_params=pltpu.CompilerParams(vmem_limit_bytes=12 << 20),
        cost_estimate=cost(3),
    )(read, *x_grid, y_grid)


def main_kernel(
    part, near, y_first, y_second, y_grid, y_test, x128, x96, x64, t128, t64, subgrid, germano,
    edge, smooth, coarse, tested, y_outer, buf_s, buf_g, sems,
):
    even = is_even("gy")
    x_grid = {128: x128, 96: x96, 64: x64}
    x_test = {128: t128, 64: t64}

    def from_neighbours(rows):
        one, two = y_first[rows, :], y_second[rows, :]
        return jnp.where(even, two, one), jnp.where(even, one, two)

    higher, lower = from_neighbours(slice(3 * QUARTER, 3 * QUARTER + 8))
    cells = lax.axis_index("gy") * NY, lax.axis_size("gy") * NY
    outer_matrix(higher, lower, *cells, y_outer)
    copies = []

    def send(buffer, out, p, sem):
        copy = pltpu.make_async_copy(buffer.at[p], out.at[p], sem)
        copy.start()
        copies.append(copy)

    for f in range(3):
        higher, lower = from_neighbours(slice(QUARTER * f, QUARTER * (f + 1)))
        for q in range(4):
            lanes = slice(HALO * q, HALO * (q + 1))
            edge[QUARTER * q : QUARTER * (q + 1), 128 * f : 128 * (f + 1)] = jnp.concatenate(
                [higher[:, lanes], jnp.zeros((QUARTER, 64), F32), lower[:, lanes]], axis=1
            )
    for start, m in VELOCITY_TILES:
        smooth[start : start + m, 0:384] = filter_x(x_grid[m], edge, start, m)
    fields = [edge[HALF : HALF + NX_COARSE, 128 * f : 128 * (f + 1)] for f in range(3)]
    products = jnp.concatenate([fields[i] * fields[j] for i, j in PAIRS], axis=1)
    for start, m in INNER_TILES:
        smooth[start : start + m, 384:] = filter_x(x_grid[m], products, start, m)

    def halo_factor(f, rows):
        hi, lo = split(smooth[0:rows, 128 * f : 128 * (f + 1)])
        return jnp.concatenate([halo_lanes(hi, lo), hi], axis=1)

    for f in range(3):
        left = halo_factor(f, NX_COARSE)
        coarse[f, :, 0:NY] = part[STARTS[f] : STARTS[f] + NX_COARSE] + times(left, y_grid[3 * NY :])
        coarse[f, :, NY:] = times(jnp.concatenate([left, near[f]], axis=1), y_outer[...])
    own = slice(HALF, HALF + NX)
    for p, (i, j) in enumerate(PAIRS):
        rows = slice(STARTS[3 + p], STARTS[3 + p] + NX)
        stress = part[rows] + times(halo_factor(3 + p, NX), y_grid[3 * NY :])
        buf_s[p] = stress - coarse[i, own, 0:NY] * coarse[j, own, 0:NY]
        send(buf_s, subgrid, p, sems.at[p])
    for f in range(9):
        field = coarse[f] if f < 3 else coarse[PAIRS[f - 3][0]] * coarse[PAIRS[f - 3][1]]
        parts = [split(filter_x(x_test[m], field, start, m)) for start, m in INNER_TILES]
        hi = jnp.concatenate([part[0] for part in parts], axis=0)
        lo = jnp.concatenate([part[1] for part in parts], axis=0)
        result = times(lanes_of(hi, lo), y_test[...])
        if f < 3:
            tested[f] = result
        else:
            i, j = PAIRS[f - 3]
            buf_g[f - 3] = result - tested[i] * tested[j]
            send(buf_g, germano, f - 3, sems.at[3 + f])
    for copy in copies:
        copy.wait()


def main(part, near, y_first, y_second, y_grid, y_test, x_parts):
    out = jax.ShapeDtypeStruct((6, NX, NY), F32)
    return pl.pallas_call(
        main_kernel,
        out_shape=[out, out],
        in_specs=[VMEM] * (6 + len(x_parts)),
        out_specs=[HBM, HBM],
        scratch_shapes=[
            pltpu.VMEM((NX_READ, 3 * 128), F32),
            pltpu.VMEM((NX_COARSE, 9 * 128), F32),
            pltpu.VMEM((3, NX_COARSE, RING), F32),
            pltpu.VMEM((3, NX, NY), F32),
            pltpu.VMEM((3 * 128, 128), BF),
            pltpu.VMEM((6, NX, NY), F32),
            pltpu.VMEM((6, NX, NY), F32),
            pltpu.SemaphoreType.DMA((12,)),
        ],
        compiler_params=pltpu.CompilerParams(vmem_limit_bytes=24 << 20),
    )(part, near, y_first, y_second, y_grid, y_test, *x_parts)


def swaps(axis, first, periodic):
    count = lax.axis_size(axis)
    last = count if periodic else count - 1
    pairs = [(i, (i + 1) % count) for i in range(first, last, 2)]
    return pairs + [(b, a) for a, b in pairs]


def local(velocity, grid_x, grid_y, test_x, test_y):
    velocity = velocity.reshape(3, NY, NX).swapaxes(1, 2)
    first, second = edges(velocity)
    x_first = lax.ppermute(first, "gx", swaps("gx", 1, True))
    x_second = lax.ppermute(second, "gx", swaps("gx", 0, True))
    y_grid, y_test, *x_parts = matrices(grid_x, test_x, grid_y.T, test_y.T)
    first, second, read = pack(velocity, x_first, x_second, grid_y.T)
    y_first = lax.ppermute(first, "gy", swaps("gy", 1, False))
    y_second = lax.ppermute(second, "gy", swaps("gy", 0, False))
    part, near = filter_own(read, x_parts[:3], y_grid)
    outs = main(part, near, y_first, y_second, y_grid, y_test, x_parts)
    return tuple(out.swapaxes(1, 2).reshape(6, 1, NY, NX) for out in outs)


def solution(mesh):
    placed = (P(None, None, "gy", "gx"), P(), P("gy", None), P(), P("gy", None))
    return jax.shard_map(
        local,
        mesh=mesh,
        in_specs=placed,
        out_specs=(P(None, None, "gy", "gx"), P(None, None, "gy", "gx")),
        check_vma=False,
    )
```

```python
import jax
import jax.numpy as jnp
from jax import lax
from jax.experimental import pallas as pl
from jax.experimental.pallas import tpu as pltpu
from jax.sharding import PartitionSpec as P

BF = jnp.bfloat16
F32 = jnp.float32
HALF = 16
TAPS = 33
HALO = 32
NX = 320
NY = 256
RING = 384
NX_READ = NX + 2 * HALO
NX_COARSE = NX + 2 * HALF
TAP_ROWS = 40
QUARTER = NX_READ // 4
PAIRS = [(0, 0), (0, 1), (0, 2), (1, 1), (1, 2), (2, 2)]
VMEM = pl.BlockSpec(memory_space=pltpu.VMEM)
SMEM = pl.BlockSpec(memory_space=pltpu.SMEM)
HBM = pl.BlockSpec(memory_space=pltpu.HBM)


def cost(us):
    return pl.CostEstimate(flops=us * 10**9, bytes_accessed=10**6, transcendentals=0)


def split(x):
    hi = x.astype(BF)
    return hi, (x - hi.astype(F32)).astype(BF)


def is_even(axis):
    return lax.rem(lax.axis_index(axis), 2) == 0


def edges(velocity):
    even = is_even("gx")
    low, high = velocity[:, :HALO], velocity[:, NX - HALO :]
    return jnp.where(even, low, high), jnp.where(even, high, low)


def pack_kernel(own, x_first, x_second, taps, first, second, read, table):
    even_x, even_y = is_even("gx"), is_even("gy")
    for f in range(3):
        read[f, HALO : HALO + NX] = own[f]
        read[f, 0:HALO] = jnp.where(even_x, x_first[f], x_second[f])
        read[f, HALO + NX :] = jnp.where(even_x, x_second[f], x_first[f])
        quarters = [pl.ds(QUARTER * q, QUARTER) for q in range(4)]
        low = jnp.concatenate([read[f, r, 0:HALO] for r in quarters], axis=1)
        high = jnp.concatenate([read[f, r, NY - HALO : NY] for r in quarters], axis=1)
        first[QUARTER * f : QUARTER * (f + 1), :] = jnp.where(even_y, low, high)
        second[QUARTER * f : QUARTER * (f + 1), :] = jnp.where(even_y, high, low)
    table[...] = jnp.zeros_like(table)
    table[0:TAPS, :] = taps[...]
    groups = [pl.ds(8 * g, 8) for g in range(TAP_ROWS // 8)]
    spare = jnp.zeros((8, 128 - 2 * TAP_ROWS), F32)
    low = jnp.concatenate([table[r, 0:HALF] for r in groups] + [spare], axis=1)
    high = jnp.concatenate([table[r, NY - HALF : NY] for r in groups] + [spare], axis=1)
    first[3 * QUARTER :, :] = jnp.where(even_y, low, high)
    second[3 * QUARTER :, :] = jnp.where(even_y, high, low)


def pack(own, x_first, x_second, taps):
    edge = jax.ShapeDtypeStruct((3 * QUARTER + 8, 128), F32)
    return pl.pallas_call(
        pack_kernel,
        out_shape=[edge, edge, jax.ShapeDtypeStruct((3, NX_READ, NY), F32)],
        in_specs=[VMEM] * 4,
        out_specs=[VMEM] * 3,
        scratch_shapes=[pltpu.VMEM((TAP_ROWS, NY), F32)],
        compiler_params=pltpu.CompilerParams(vmem_limit_bytes=8 << 20),
        cost_estimate=cost(5),
    )(own, x_first, x_second, taps)


def norm_y(taps, cell, total_cells):
    tap = lax.broadcasted_iota(jnp.int32, taps.shape, 0)
    source = cell + tap - HALF
    masked = jnp.where((source >= 0) & (source < total_cells) & (tap < TAPS), taps, 0.0)
    total = jnp.sum(masked, axis=0, keepdims=True)
    weights = masked / jnp.where(total > 0, total, 1.0)
    high = weights.astype(BF).astype(F32)
    return high, weights - high


def slanted(part, rows, cells):
    x = jnp.concatenate([part, jnp.zeros((rows - part.shape[0], 128), F32)], axis=0)
    lane = lax.broadcasted_iota(jnp.int32, x.shape, 1)
    step = 1
    while step < cells:
        x = jnp.where((lane & step) != 0, pltpu.roll(x, step, 0), x)
        step *= 2
    return x


def rolled(part, offset, lanes):
    m = part.shape[0]
    wide = jnp.concatenate([part, jnp.zeros((m, lanes - 128), F32)], axis=1)
    return pltpu.roll(wide, offset % lanes, 1, stride=1, stride_axis=0)


def y_matrix(taps_ref, first_cell, total_cells, table, out):
    table[...] = jnp.zeros_like(table)
    table[0:TAPS, :] = taps_ref[...]
    out[...] = jnp.zeros_like(out)
    for s in (0, 128):
        cell = first_cell + s + lax.broadcasted_iota(jnp.int32, (TAP_ROWS, 128), 1)
        weights = norm_y(table[:, s : s + 128], cell, total_cells)
        hi, lo = (slanted(part, 128 + 2 * HALF, 128).astype(BF) for part in weights)
        own = slice(HALF, 128 + 2 * HALF) if s == 0 else slice(0, 128 + HALF)
        halo = slice(0, HALF) if s == 0 else slice(128 + HALF, 128 + 2 * HALF)
        row = 0 if s == 0 else 128 - HALF
        halo_row = 128 - HALF if s == 0 else 0
        lanes = slice(s, s + 128)
        for base, part in ((0, hi), (NY, hi), (2 * NY, lo)):
            out[base + row : base + row + 128 + HALF, lanes] = part[own]
        for base, part in ((halo_row, hi), ((halo_row + 64) % 128, hi), (128 + halo_row, lo)):
            out[3 * NY + base : 3 * NY + base + HALF, lanes] = part[halo]


def outer_matrix(higher, lower, first_cell, total_cells, out):
    lane = lax.broadcasted_iota(jnp.int32, (TAP_ROWS, 128), 1)
    groups = [slice(HALF * g, HALF * (g + 1)) for g in range(TAP_ROWS // 8)]
    spare = jnp.zeros((8, 128 - 2 * HALF), F32)
    taps = [jnp.concatenate([higher[:, g], spare, lower[:, g]], axis=1) for g in groups]
    cell = first_cell + jnp.where(lane < 64, NY + lane, lane - 128)
    weights = norm_y(jnp.concatenate(taps, axis=0), cell, total_cells)
    hi, lo = (slanted(part, 3 * HALF, HALF) for part in weights)
    low_side = lax.broadcasted_iota(jnp.int32, hi.shape, 1) >= 64
    out[...] = jnp.zeros_like(out)
    ends = []
    for part in (hi, lo):
        high_end = jnp.where(low_side, 0.0, part).astype(BF)
        low_end = jnp.where(low_side, part, 0.0).astype(BF)
        ends.append((high_end[HALF:], low_end[0:HALO], high_end[0:HALF], low_end[HALO:]))
    for base, part in ((0, 0), (64, 0), (128, 1)):
        out[base : base + HALO, :] = ends[part][0]
    for base, part in ((96, 0), (32, 0), (128 + 96, 1)):
        out[base : base + HALO, :] = ends[part][1]
    for base, part in ((112, 0), (16, 0), (48, 1)):
        out[256 + base : 256 + base + HALF, :] = ends[part][2]
    for base, part in ((0, 0), (32, 0), (64, 1)):
        out[256 + base : 256 + base + HALF, :] = ends[part][3]


def halo_lanes(hi, lo):
    lane = lax.broadcasted_iota(jnp.int32, hi.shape, 1)
    outer = (lane < HALO) | (lane >= 128 - HALO)
    return jnp.where(outer, hi, pltpu.roll(lo.astype(F32), 64, 1).astype(BF))


def lanes_of(hi, lo):
    own = [hi[:, :NY], lo[:, :NY], hi[:, :NY]]
    return jnp.concatenate(own + [halo_lanes(hi[:, NY:], lo[:, NY:]), hi[:, NY:]], axis=1)


def times(left, matrix):
    return jnp.dot(left, matrix, preferred_element_type=F32)


def x_taps(taps_ref, rows):
    lane = lax.broadcasted_iota(jnp.int32, (rows, 128), 1)
    taps = jnp.zeros((rows, 128), F32)
    for t in range(TAPS):
        taps = jnp.where(lane == t, taps_ref[t], taps)
    return taps / jnp.sum(taps, axis=1, keepdims=True)


def x_matrix(taps_ref, m):
    k = m + 2 * HALF
    lanes = -(-3 * k // 128) * 128
    taps = x_taps(taps_ref, m)
    high = taps.astype(BF).astype(F32)
    low = taps - high
    total = rolled(high, 0, lanes) + rolled(high, k, lanes) + rolled(low, 2 * k, lanes)
    return total.astype(BF)


def filter_x(matrix, x, start, m):
    k = m + 2 * HALF
    hi, lo = split(x[start : start + k])
    spare = matrix.shape[1] - 3 * k
    parts = [hi, lo, hi]
    if spare:
        parts.append(jnp.zeros((spare, x.shape[1]), BF))
    return jnp.dot(matrix[...], jnp.concatenate(parts, axis=0), preferred_element_type=F32)


def matrix_kernel(grid_x, test_x, grid_y, test_y, y_grid, y_test, *rest):
    first_cell = lax.axis_index("gy") * NY
    total_cells = lax.axis_size("gy") * NY
    table = rest[-1]
    for out, (taps, m) in zip(rest[:-1], X_PARTS):
        out[...] = x_matrix((grid_x, test_x)[taps], m)
    y_matrix(grid_y, first_cell, total_cells, table, y_grid)
    y_matrix(test_y, first_cell, total_cells, table, y_test)


X_PARTS = [(0, 128), (0, 96), (0, 64), (1, 128), (1, 64)]


def matrices(grid_x, test_x, grid_y, test_y):
    return pl.pallas_call(
        matrix_kernel,
        out_shape=[
            jax.ShapeDtypeStruct((4 * NY, NY), BF),
            jax.ShapeDtypeStruct((4 * NY, NY), BF),
        ]
        + [jax.ShapeDtypeStruct((m, -(-3 * (m + 2 * HALF) // 128) * 128), BF) for _, m in X_PARTS],
        in_specs=[SMEM, SMEM, VMEM, VMEM],
        out_specs=[VMEM] * (2 + len(X_PARTS)),
        scratch_shapes=[pltpu.VMEM((TAP_ROWS, NY), F32)],
        compiler_params=pltpu.CompilerParams(vmem_limit_bytes=61 << 20),
        cost_estimate=cost(2),
    )(grid_x, test_x, grid_y, test_y)


VELOCITY_TILES = ((0, 128), (128, 128), (256, 96))
INNER_TILES = ((0, 128), (128, 128), (256, 64))


STARTS = [NX_COARSE * f for f in range(3)] + [3 * NX_COARSE + NX * p for p in range(6)]
STACK = 3 * NX_COARSE + 6 * NX


def own_kernel(read, x128, x96, x64, y_grid, part, near, hi, lo):
    x_grid = {128: x128, 96: x96, 64: x64}
    for f in range(9):
        if f < 3:
            field, tiles = read[f], VELOCITY_TILES
        else:
            i, j = PAIRS[f - 3]
            inner = slice(HALF, HALF + NX_COARSE)
            field, tiles = read[i, inner] * read[j, inner], INNER_TILES
        for start, m in tiles:
            rows = slice(STARTS[f] + start, STARTS[f] + start + m)
            hi[rows], lo[rows] = split(filter_x(x_grid[m], field, start, m))
        rows = slice(STARTS[f], STARTS[f] + (NX_COARSE if f < 3 else NX))
        if f < 3:
            near[f] = near_lanes(hi[rows], lo[rows])
    part[...] = times(jnp.concatenate([hi[...], lo[...], hi[...]], axis=1), y_grid[0 : 3 * NY])


def near_lanes(hi, lo):
    lane = lax.broadcasted_iota(jnp.int32, (hi.shape[0], 128), 1)
    ends = [jnp.where(lane < HALF, x[:, 0:128], x[:, 128:NY]).astype(F32) for x in (hi, lo)]
    low, again = pltpu.roll(ends[1], 32, 1), pltpu.roll(ends[0], 64, 1)
    ends = jnp.where((lane < HALF) | (lane >= 128 - HALF), ends[0], jnp.where(lane < 48, low, again))
    return ends.astype(BF)


def filter_own(read, x_grid, y_grid):
    return pl.pallas_call(
        own_kernel,
        out_shape=[
            jax.ShapeDtypeStruct((STACK, NY), F32),
            jax.ShapeDtypeStruct((3, NX_COARSE, 128), BF),
        ],
        in_specs=[VMEM] * 5,
        out_specs=[VMEM] * 2,
        scratch_shapes=[pltpu.VMEM((STACK, NY), BF), pltpu.VMEM((STACK, NY), BF)],
        compiler_params=pltpu.CompilerParams(vmem_limit_bytes=12 << 20),
        cost_estimate=cost(3),
    )(read, *x_grid, y_grid)


def main_kernel(
    part, near, y_first, y_second, y_grid, y_test, x128, x96, x64, t128, t64, subgrid, germano,
    edge, smooth, coarse, tested, y_outer, buf_s, buf_g, own_hi, own_lo, halo, sems,
):
    even = is_even("gy")
    x_grid = {128: x128, 96: x96, 64: x64}
    x_test = {128: t128, 64: t64}

    def from_neighbours(rows):
        one, two = y_first[rows, :], y_second[rows, :]
        return jnp.where(even, two, one), jnp.where(even, one, two)

    higher, lower = from_neighbours(slice(3 * QUARTER, 3 * QUARTER + 8))
    cells = lax.axis_index("gy") * NY, lax.axis_size("gy") * NY
    outer_matrix(higher, lower, *cells, y_outer)
    copies = []

    def send(buffer, out, p, sem):
        copy = pltpu.make_async_copy(buffer.at[p], out.at[p], sem)
        copy.start()
        copies.append(copy)

    for f in range(3):
        higher, lower = from_neighbours(slice(QUARTER * f, QUARTER * (f + 1)))
        for q in range(4):
            lanes = slice(HALO * q, HALO * (q + 1))
            edge[QUARTER * q : QUARTER * (q + 1), 128 * f : 128 * (f + 1)] = jnp.concatenate(
                [higher[:, lanes], jnp.zeros((QUARTER, 64), F32), lower[:, lanes]], axis=1
            )
    for start, m in VELOCITY_TILES:
        smooth[start : start + m, 0:384] = filter_x(x_grid[m], edge, start, m)
    fields = [edge[HALF : HALF + NX_COARSE, 128 * f : 128 * (f + 1)] for f in range(3)]
    products = jnp.concatenate([fields[i] * fields[j] for i, j in PAIRS], axis=1)
    for start, m in INNER_TILES:
        smooth[start : start + m, 384:] = filter_x(x_grid[m], products, start, m)

    def halo_factor(f, rows):
        hi, lo = split(smooth[0:rows, 128 * f : 128 * (f + 1)])
        return jnp.concatenate([halo_lanes(hi, lo), hi], axis=1)

    for f in range(3):
        left = halo_factor(f, NX_COARSE)
        coarse[f, :, 0:NY] = part[STARTS[f] : STARTS[f] + NX_COARSE] + times(left, y_grid[3 * NY :])
        coarse[f, :, NY:] = times(jnp.concatenate([left, near[f]], axis=1), y_outer[...])
    own = slice(HALF, HALF + NX)
    for p, (i, j) in enumerate(PAIRS):
        rows = slice(STARTS[3 + p], STARTS[3 + p] + NX)
        stress = part[rows] + times(halo_factor(3 + p, NX), y_grid[3 * NY :])
        buf_s[p] = stress - coarse[i, own, 0:NY] * coarse[j, own, 0:NY]
        send(buf_s, subgrid, p, sems.at[p])
    for f in range(9):
        field = coarse[f] if f < 3 else coarse[PAIRS[f - 3][0]] * coarse[PAIRS[f - 3][1]]
        for start, m in INNER_TILES:
            rows = slice(NX * f + start, NX * f + start + m)
            hi, lo = split(filter_x(x_test[m], field, start, m))
            own_hi[rows], own_lo[rows] = hi[:, :NY], lo[:, :NY]
            halo[rows] = jnp.concatenate([halo_lanes(hi[:, NY:], lo[:, NY:]), hi[:, NY:]], axis=1)
    for first, last in ((0, 3), (3, 6), (6, 9)):
        rows = slice(NX * first, NX * last)
        left = jnp.concatenate([own_hi[rows], own_lo[rows], own_hi[rows], halo[rows]], axis=1)
        results = times(left, y_test[...])
        for f in range(first, last):
            result = results[NX * (f - first) : NX * (f - first + 1)]
            if f < 3:
                tested[f] = result
            else:
                i, j = PAIRS[f - 3]
                buf_g[f - 3] = result - tested[i] * tested[j]
                send(buf_g, germano, f - 3, sems.at[3 + f])
    for copy in copies:
        copy.wait()


def main(part, near, y_first, y_second, y_grid, y_test, x_parts):
    out = jax.ShapeDtypeStruct((6, NX, NY), F32)
    return pl.pallas_call(
        main_kernel,
        out_shape=[out, out],
        in_specs=[VMEM] * (6 + len(x_parts)),
        out_specs=[HBM, HBM],
        scratch_shapes=[
            pltpu.VMEM((NX_READ, 3 * 128), F32),
            pltpu.VMEM((NX_COARSE, 9 * 128), F32),
            pltpu.VMEM((3, NX_COARSE, RING), F32),
            pltpu.VMEM((3, NX, NY), F32),
            pltpu.VMEM((3 * 128, 128), BF),
            pltpu.VMEM((6, NX, NY), F32),
            pltpu.VMEM((6, NX, NY), F32),
            pltpu.VMEM((9 * NX, NY), BF),
            pltpu.VMEM((9 * NX, NY), BF),
            pltpu.VMEM((9 * NX, NY), BF),
            pltpu.SemaphoreType.DMA((12,)),
        ],
        compiler_params=pltpu.CompilerParams(vmem_limit_bytes=24 << 20),
    )(part, near, y_first, y_second, y_grid, y_test, *x_parts)


def swaps(axis, first, periodic):
    count = lax.axis_size(axis)
    last = count if periodic else count - 1
    pairs = [(i, (i + 1) % count) for i in range(first, last, 2)]
    return pairs + [(b, a) for a, b in pairs]


def local(velocity, grid_x, grid_y, test_x, test_y):
    velocity = velocity.reshape(3, NY, NX).swapaxes(1, 2)
    first, second = edges(velocity)
    x_first = lax.ppermute(first, "gx", swaps("gx", 1, True))
    x_second = lax.ppermute(second, "gx", swaps("gx", 0, True))
    y_grid, y_test, *x_parts = matrices(grid_x, test_x, grid_y.T, test_y.T)
    first, second, read = pack(velocity, x_first, x_second, grid_y.T)
    y_first = lax.ppermute(first, "gy", swaps("gy", 1, False))
    y_second = lax.ppermute(second, "gy", swaps("gy", 0, False))
    part, near = filter_own(read, x_parts[:3], y_grid)
    outs = main(part, near, y_first, y_second, y_grid, y_test, x_parts)
    return tuple(out.swapaxes(1, 2).reshape(6, 1, NY, NX) for out in outs)


def solution(mesh):
    placed = (P(None, None, "gy", "gx"), P(), P("gy", None), P(), P("gy", None))
    return jax.shard_map(
        local,
        mesh=mesh,
        in_specs=placed,
        out_specs=(P(None, None, "gy", "gx"), P(None, None, "gy", "gx")),
        check_vma=False,
    )
```

```python
import jax
import jax.numpy as jnp
from jax import lax
from jax.experimental import pallas as pl
from jax.experimental.pallas import tpu as pltpu
from jax.sharding import PartitionSpec as P

BF = jnp.bfloat16
F32 = jnp.float32
HALF = 16
TAPS = 33
HALO = 32
NX = 320
NY = 256
RING = 384
NX_READ = NX + 2 * HALO
NX_COARSE = NX + 2 * HALF
TAP_ROWS = 40
QUARTER = NX_READ // 4
PAIRS = [(0, 0), (0, 1), (0, 2), (1, 1), (1, 2), (2, 2)]
VMEM = pl.BlockSpec(memory_space=pltpu.VMEM)
SMEM = pl.BlockSpec(memory_space=pltpu.SMEM)
HBM = pl.BlockSpec(memory_space=pltpu.HBM)


def cost(us):
    return pl.CostEstimate(flops=us * 10**9, bytes_accessed=10**6, transcendentals=0)


def split(x):
    hi = x.astype(BF)
    return hi, (x - hi.astype(F32)).astype(BF)


def is_even(axis):
    return lax.rem(lax.axis_index(axis), 2) == 0


def edges(velocity):
    even = is_even("gx")
    low, high = velocity[:, :HALO], velocity[:, NX - HALO :]
    return jnp.where(even, low, high), jnp.where(even, high, low)


def pack_kernel(own, x_first, x_second, taps, first, second, read, table):
    even_x, even_y = is_even("gx"), is_even("gy")
    for f in range(3):
        read[f, HALO : HALO + NX] = own[f]
        read[f, 0:HALO] = jnp.where(even_x, x_first[f], x_second[f])
        read[f, HALO + NX :] = jnp.where(even_x, x_second[f], x_first[f])
        quarters = [pl.ds(QUARTER * q, QUARTER) for q in range(4)]
        low = jnp.concatenate([read[f, r, 0:HALO] for r in quarters], axis=1)
        high = jnp.concatenate([read[f, r, NY - HALO : NY] for r in quarters], axis=1)
        first[QUARTER * f : QUARTER * (f + 1), :] = jnp.where(even_y, low, high)
        second[QUARTER * f : QUARTER * (f + 1), :] = jnp.where(even_y, high, low)
    table[...] = jnp.zeros_like(table)
    table[0:TAPS, :] = taps[...]
    groups = [pl.ds(8 * g, 8) for g in range(TAP_ROWS // 8)]
    spare = jnp.zeros((8, 128 - 2 * TAP_ROWS), F32)
    low = jnp.concatenate([table[r, 0:HALF] for r in groups] + [spare], axis=1)
    high = jnp.concatenate([table[r, NY - HALF : NY] for r in groups] + [spare], axis=1)
    first[3 * QUARTER :, :] = jnp.where(even_y, low, high)
    second[3 * QUARTER :, :] = jnp.where(even_y, high, low)


def pack(own, x_first, x_second, taps):
    edge = jax.ShapeDtypeStruct((3 * QUARTER + 8, 128), F32)
    return pl.pallas_call(
        pack_kernel,
        out_shape=[edge, edge, jax.ShapeDtypeStruct((3, NX_READ, NY), F32)],
        in_specs=[VMEM] * 4,
        out_specs=[VMEM] * 3,
        scratch_shapes=[pltpu.VMEM((TAP_ROWS, NY), F32)],
        compiler_params=pltpu.CompilerParams(vmem_limit_bytes=8 << 20),
        cost_estimate=cost(5),
    )(own, x_first, x_second, taps)


def norm_y(taps, cell, total_cells):
    tap = lax.broadcasted_iota(jnp.int32, taps.shape, 0)
    source = cell + tap - HALF
    masked = jnp.where((source >= 0) & (source < total_cells) & (tap < TAPS), taps, 0.0)
    total = jnp.sum(masked, axis=0, keepdims=True)
    weights = masked / jnp.where(total > 0, total, 1.0)
    high = weights.astype(BF).astype(F32)
    return high, weights - high


def slanted(part, rows, cells):
    x = jnp.concatenate([part, jnp.zeros((rows - part.shape[0], 128), F32)], axis=0)
    lane = lax.broadcasted_iota(jnp.int32, x.shape, 1)
    step = 1
    while step < cells:
        x = jnp.where((lane & step) != 0, pltpu.roll(x, step, 0), x)
        step *= 2
    return x


def rolled(part, offset, lanes):
    m = part.shape[0]
    wide = jnp.concatenate([part, jnp.zeros((m, lanes - 128), F32)], axis=1)
    return pltpu.roll(wide, offset % lanes, 1, stride=1, stride_axis=0)


def y_matrix(taps_ref, first_cell, total_cells, table, out):
    table[...] = jnp.zeros_like(table)
    table[0:TAPS, :] = taps_ref[...]
    out[...] = jnp.zeros_like(out)
    for s in (0, 128):
        cell = first_cell + s + lax.broadcasted_iota(jnp.int32, (TAP_ROWS, 128), 1)
        weights = norm_y(table[:, s : s + 128], cell, total_cells)
        hi, lo = (slanted(part, 128 + 2 * HALF, 128).astype(BF) for part in weights)
        own = slice(HALF, 128 + 2 * HALF) if s == 0 else slice(0, 128 + HALF)
        halo = slice(0, HALF) if s == 0 else slice(128 + HALF, 128 + 2 * HALF)
        row = 0 if s == 0 else 128 - HALF
        halo_row = 128 - HALF if s == 0 else 0
        lanes = slice(s, s + 128)
        for base, part in ((0, hi), (NY, hi), (2 * NY, lo)):
            out[base + row : base + row + 128 + HALF, lanes] = part[own]
        for base, part in ((halo_row, hi), ((halo_row + 64) % 128, hi), (128 + halo_row, lo)):
            out[3 * NY + base : 3 * NY + base + HALF, lanes] = part[halo]


def outer_matrix(higher, lower, first_cell, total_cells, out):
    lane = lax.broadcasted_iota(jnp.int32, (TAP_ROWS, 128), 1)
    groups = [slice(HALF * g, HALF * (g + 1)) for g in range(TAP_ROWS // 8)]
    spare = jnp.zeros((8, 128 - 2 * HALF), F32)
    taps = [jnp.concatenate([higher[:, g], spare, lower[:, g]], axis=1) for g in groups]
    cell = first_cell + jnp.where(lane < 64, NY + lane, lane - 128)
    weights = norm_y(jnp.concatenate(taps, axis=0), cell, total_cells)
    hi, lo = (slanted(part, 3 * HALF, HALF) for part in weights)
    low_side = lax.broadcasted_iota(jnp.int32, hi.shape, 1) >= 64
    out[...] = jnp.zeros_like(out)
    ends = []
    for part in (hi, lo):
        high_end = jnp.where(low_side, 0.0, part).astype(BF)
        low_end = jnp.where(low_side, part, 0.0).astype(BF)
        ends.append((high_end[HALF:], low_end[0:HALO], high_end[0:HALF], low_end[HALO:]))
    for base, part in ((0, 0), (64, 0), (128, 1)):
        out[base : base + HALO, :] = ends[part][0]
    for base, part in ((96, 0), (32, 0), (128 + 96, 1)):
        out[base : base + HALO, :] = ends[part][1]
    for base, part in ((112, 0), (16, 0), (48, 1)):
        out[256 + base : 256 + base + HALF, :] = ends[part][2]
    for base, part in ((0, 0), (32, 0), (64, 1)):
        out[256 + base : 256 + base + HALF, :] = ends[part][3]


def halo_lanes(hi, lo):
    lane = lax.broadcasted_iota(jnp.int32, hi.shape, 1)
    outer = (lane < HALO) | (lane >= 128 - HALO)
    return jnp.where(outer, hi, pltpu.roll(lo.astype(F32), 64, 1).astype(BF))


def packed(tiles):
    total = tiles[0]
    for q, tile in enumerate(tiles[1:], 1):
        total = total + pltpu.roll(tile, HALO * q, 1)
    return total


def unpacked(tile, count):
    hi, lo = (part.astype(F32) for part in split(tile))
    lane = lax.broadcasted_iota(jnp.int32, tile.shape, 1)
    outer = (lane < HALO) | (lane >= 128 - HALO)
    factors = []
    for q in range(count):
        high = pltpu.roll(hi, 128 - HALO * q, 1) if q else hi
        low = pltpu.roll(lo, (64 - HALO * q) % 128, 1) if q != 2 else lo
        factors.append(jnp.concatenate([jnp.where(outer, high, low), high], axis=1).astype(BF))
    return factors


def times(left, matrix):
    return jnp.dot(left, matrix, preferred_element_type=F32)


def x_taps(taps_ref, rows):
    lane = lax.broadcasted_iota(jnp.int32, (rows, 128), 1)
    taps = jnp.zeros((rows, 128), F32)
    for t in range(TAPS):
        taps = jnp.where(lane == t, taps_ref[t], taps)
    return taps / jnp.sum(taps, axis=1, keepdims=True)


def x_matrix(taps_ref, m):
    k = m + 2 * HALF
    lanes = -(-3 * k // 128) * 128
    taps = x_taps(taps_ref, m)
    high = taps.astype(BF).astype(F32)
    low = taps - high
    total = rolled(high, 0, lanes) + rolled(high, k, lanes) + rolled(low, 2 * k, lanes)
    return total.astype(BF)


def filter_x(matrix, x, start, m):
    k = m + 2 * HALF
    hi, lo = split(x[start : start + k])
    spare = matrix.shape[1] - 3 * k
    parts = [hi, lo, hi]
    if spare:
        parts.append(jnp.zeros((spare, x.shape[1]), BF))
    return jnp.dot(matrix[...], jnp.concatenate(parts, axis=0), preferred_element_type=F32)


def matrix_kernel(grid_x, test_x, grid_y, test_y, y_grid, y_test, *rest):
    first_cell = lax.axis_index("gy") * NY
    total_cells = lax.axis_size("gy") * NY
    table = rest[-1]
    for out, (taps, m) in zip(rest[:-1], X_PARTS):
        out[...] = x_matrix((grid_x, test_x)[taps], m)
    y_matrix(grid_y, first_cell, total_cells, table, y_grid)
    y_matrix(test_y, first_cell, total_cells, table, y_test)


X_PARTS = [(0, 128), (0, 96), (0, 64), (1, 128), (1, 64)]


def matrices(grid_x, test_x, grid_y, test_y):
    return pl.pallas_call(
        matrix_kernel,
        out_shape=[
            jax.ShapeDtypeStruct((4 * NY, NY), BF),
            jax.ShapeDtypeStruct((4 * NY, NY), BF),
        ]
        + [jax.ShapeDtypeStruct((m, -(-3 * (m + 2 * HALF) // 128) * 128), BF) for _, m in X_PARTS],
        in_specs=[SMEM, SMEM, VMEM, VMEM],
        out_specs=[VMEM] * (2 + len(X_PARTS)),
        scratch_shapes=[pltpu.VMEM((TAP_ROWS, NY), F32)],
        compiler_params=pltpu.CompilerParams(vmem_limit_bytes=61 << 20),
        cost_estimate=cost(2),
    )(grid_x, test_x, grid_y, test_y)


VELOCITY_TILES = ((0, 128), (128, 128), (256, 96))
INNER_TILES = ((0, 128), (128, 128), (256, 64))


STARTS = [NX_COARSE * f for f in range(3)] + [3 * NX_COARSE + NX * p for p in range(6)]
STACK = 3 * NX_COARSE + 6 * NX


def own_kernel(read, x128, x96, x64, y_grid, part, near, hi, lo):
    x_grid = {128: x128, 96: x96, 64: x64}
    for f in range(9):
        if f < 3:
            field, tiles = read[f], VELOCITY_TILES
        else:
            i, j = PAIRS[f - 3]
            inner = slice(HALF, HALF + NX_COARSE)
            field, tiles = read[i, inner] * read[j, inner], INNER_TILES
        for start, m in tiles:
            rows = slice(STARTS[f] + start, STARTS[f] + start + m)
            hi[rows], lo[rows] = split(filter_x(x_grid[m], field, start, m))
        rows = slice(STARTS[f], STARTS[f] + (NX_COARSE if f < 3 else NX))
        if f < 3:
            near[f] = near_lanes(hi[rows], lo[rows])
    part[...] = times(jnp.concatenate([hi[...], lo[...], hi[...]], axis=1), y_grid[0 : 3 * NY])


def near_lanes(hi, lo):
    lane = lax.broadcasted_iota(jnp.int32, (hi.shape[0], 128), 1)
    ends = [jnp.where(lane < HALF, x[:, 0:128], x[:, 128:NY]).astype(F32) for x in (hi, lo)]
    low, again = pltpu.roll(ends[1], 32, 1), pltpu.roll(ends[0], 64, 1)
    ends = jnp.where((lane < HALF) | (lane >= 128 - HALF), ends[0], jnp.where(lane < 48, low, again))
    return ends.astype(BF)


def filter_own(read, x_grid, y_grid):
    return pl.pallas_call(
        own_kernel,
        out_shape=[
            jax.ShapeDtypeStruct((STACK, NY), F32),
            jax.ShapeDtypeStruct((3, NX_COARSE, 128), BF),
        ],
        in_specs=[VMEM] * 5,
        out_specs=[VMEM] * 2,
        scratch_shapes=[pltpu.VMEM((STACK, NY), BF), pltpu.VMEM((STACK, NY), BF)],
        compiler_params=pltpu.CompilerParams(vmem_limit_bytes=12 << 20),
        cost_estimate=cost(3),
    )(read, *x_grid, y_grid)


def main_kernel(
    part, ends, y_first, y_second, y_grid, y_test, x128, x96, x64, t128, t64, subgrid, germano,
    edge, smooth, coarse, tested, y_outer, buf_s, buf_g, own_hi, own_lo, halo, sems,
):
    even = is_even("gy")
    x_grid = {128: x128, 96: x96, 64: x64}
    x_test = {128: t128, 64: t64}

    def from_neighbours(rows):
        one, two = y_first[rows, :], y_second[rows, :]
        return jnp.where(even, two, one), jnp.where(even, one, two)

    higher, lower = from_neighbours(slice(3 * QUARTER, 3 * QUARTER + 8))
    cells = lax.axis_index("gy") * NY, lax.axis_size("gy") * NY
    outer_matrix(higher, lower, *cells, y_outer)
    copies = []

    def send(buffer, out, p, sem):
        copy = pltpu.make_async_copy(buffer.at[p], out.at[p], sem)
        copy.start()
        copies.append(copy)

    for f in range(3):
        higher, lower = from_neighbours(slice(QUARTER * f, QUARTER * (f + 1)))
        for q in range(4):
            lanes = slice(HALO * q, HALO * (q + 1))
            edge[QUARTER * q : QUARTER * (q + 1), 128 * f : 128 * (f + 1)] = jnp.concatenate(
                [higher[:, lanes], jnp.zeros((QUARTER, 64), F32), lower[:, lanes]], axis=1
            )
    for start, m in VELOCITY_TILES:
        smooth[start : start + m, 0:384] = filter_x(x_grid[m], edge, start, m)
    lane = lax.broadcasted_iota(jnp.int32, (NX_COARSE, 128), 1)
    near = (lane < HALF) | (lane >= 128 - HALF)
    fields = [edge[HALF : HALF + NX_COARSE, 128 * f : 128 * (f + 1)] for f in range(3)]
    fields = [jnp.where(near, field, 0.0) for field in fields]
    products = [fields[i] * fields[j] for i, j in PAIRS]
    products = jnp.concatenate([packed(products[0:4]), packed(products[4:6])], axis=1)
    for start, m in INNER_TILES:
        smooth[start : start + m, 384:] = filter_x(x_grid[m], products, start, m)

    def halo_factor(f, rows):
        hi, lo = split(smooth[0:rows, 128 * f : 128 * (f + 1)])
        return jnp.concatenate([halo_lanes(hi, lo), hi], axis=1)

    for f in range(3):
        left = halo_factor(f, NX_COARSE)
        coarse[f, :, 0:NY] = part[STARTS[f] : STARTS[f] + NX_COARSE] + times(left, y_grid[3 * NY :])
        coarse[f, :, NY:] = times(jnp.concatenate([left, ends[f]], axis=1), y_outer[...])
    own = slice(HALF, HALF + NX)
    factors = unpacked(smooth[0:NX, 384:512], 4) + unpacked(smooth[0:NX, 512:640], 2)
    for p, (i, j) in enumerate(PAIRS):
        rows = slice(STARTS[3 + p], STARTS[3 + p] + NX)
        stress = part[rows] + times(factors[p], y_grid[3 * NY :])
        buf_s[p] = stress - coarse[i, own, 0:NY] * coarse[j, own, 0:NY]
        send(buf_s, subgrid, p, sems.at[p])
    def test_field(f, lanes):
        if f < 3:
            return coarse[f, :, lanes]
        i, j = PAIRS[f - 3]
        return coarse[i, :, lanes] * coarse[j, :, lanes]

    groups = [range(0, 4), range(4, 8), range(8, 9)]
    halos = [packed([test_field(f, slice(NY, RING)) for f in group]) for group in groups]
    halos = jnp.concatenate(halos, axis=1)
    for start, m in INNER_TILES:
        smooth[start : start + m, 0:384] = filter_x(x_test[m], halos, start, m)
    for n, group in enumerate(groups):
        for f, factor in zip(group, unpacked(smooth[0:NX, 128 * n : 128 * (n + 1)], len(group))):
            halo[NX * f : NX * (f + 1)] = factor
    for f in range(9):
        field = test_field(f, slice(0, NY))
        for start, m in INNER_TILES:
            rows = slice(NX * f + start, NX * f + start + m)
            own_hi[rows], own_lo[rows] = split(filter_x(x_test[m], field, start, m))
    for first, last in ((0, 3), (3, 6), (6, 9)):
        rows = slice(NX * first, NX * last)
        left = jnp.concatenate([own_hi[rows], own_lo[rows], own_hi[rows], halo[rows]], axis=1)
        results = times(left, y_test[...])
        for f in range(first, last):
            result = results[NX * (f - first) : NX * (f - first + 1)]
            if f < 3:
                tested[f] = result
            else:
                i, j = PAIRS[f - 3]
                buf_g[f - 3] = result - tested[i] * tested[j]
                send(buf_g, germano, f - 3, sems.at[3 + f])
    for copy in copies:
        copy.wait()


def main(part, near, y_first, y_second, y_grid, y_test, x_parts):
    out = jax.ShapeDtypeStruct((6, NX, NY), F32)
    return pl.pallas_call(
        main_kernel,
        out_shape=[out, out],
        in_specs=[VMEM] * (6 + len(x_parts)),
        out_specs=[HBM, HBM],
        scratch_shapes=[
            pltpu.VMEM((NX_READ, 3 * 128), F32),
            pltpu.VMEM((NX_COARSE, 5 * 128), F32),
            pltpu.VMEM((3, NX_COARSE, RING), F32),
            pltpu.VMEM((3, NX, NY), F32),
            pltpu.VMEM((3 * 128, 128), BF),
            pltpu.VMEM((6, NX, NY), F32),
            pltpu.VMEM((6, NX, NY), F32),
            pltpu.VMEM((9 * NX, NY), BF),
            pltpu.VMEM((9 * NX, NY), BF),
            pltpu.VMEM((9 * NX, NY), BF),
            pltpu.SemaphoreType.DMA((12,)),
        ],
        compiler_params=pltpu.CompilerParams(vmem_limit_bytes=24 << 20),
    )(part, near, y_first, y_second, y_grid, y_test, *x_parts)


def swaps(axis, first, periodic):
    count = lax.axis_size(axis)
    last = count if periodic else count - 1
    pairs = [(i, (i + 1) % count) for i in range(first, last, 2)]
    return pairs + [(b, a) for a, b in pairs]


def local(velocity, grid_x, grid_y, test_x, test_y):
    velocity = velocity.reshape(3, NY, NX).swapaxes(1, 2)
    first, second = edges(velocity)
    x_first = lax.ppermute(first, "gx", swaps("gx", 1, True))
    x_second = lax.ppermute(second, "gx", swaps("gx", 0, True))
    y_grid, y_test, *x_parts = matrices(grid_x, test_x, grid_y.T, test_y.T)
    first, second, read = pack(velocity, x_first, x_second, grid_y.T)
    y_first = lax.ppermute(first, "gy", swaps("gy", 1, False))
    y_second = lax.ppermute(second, "gy", swaps("gy", 0, False))
    part, near = filter_own(read, x_parts[:3], y_grid)
    outs = main(part, near, y_first, y_second, y_grid, y_test, x_parts)
    return tuple(out.swapaxes(1, 2).reshape(6, 1, NY, NX) for out in outs)


def solution(mesh):
    placed = (P(None, None, "gy", "gx"), P(), P("gy", None), P(), P("gy", None))
    return jax.shard_map(
        local,
        mesh=mesh,
        in_specs=placed,
        out_specs=(P(None, None, "gy", "gx"), P(None, None, "gy", "gx")),
        check_vma=False,
    )
```

```python
import jax
import jax.numpy as jnp
from jax import lax
from jax.experimental import pallas as pl
from jax.experimental.pallas import tpu as pltpu
from jax.sharding import PartitionSpec as P

BF = jnp.bfloat16
F32 = jnp.float32
HALF = 16
TAPS = 33
HALO = 32
NX = 320
NY = 256
RING = 384
NX_READ = NX + 2 * HALO
NX_COARSE = NX + 2 * HALF
TAP_ROWS = 40
QUARTER = NX_READ // 4
PAIRS = [(0, 0), (0, 1), (0, 2), (1, 1), (1, 2), (2, 2)]
VMEM = pl.BlockSpec(memory_space=pltpu.VMEM)
SMEM = pl.BlockSpec(memory_space=pltpu.SMEM)
HBM = pl.BlockSpec(memory_space=pltpu.HBM)


def cost(us):
    return pl.CostEstimate(flops=us * 10**9, bytes_accessed=10**6, transcendentals=0)


def split(x):
    hi = x.astype(BF)
    return hi, (x - hi.astype(F32)).astype(BF)


def is_even(axis):
    return lax.rem(lax.axis_index(axis), 2) == 0


def edges(velocity):
    even = is_even("gx")
    low, high = velocity[:, :HALO], velocity[:, NX - HALO :]
    return jnp.where(even, low, high), jnp.where(even, high, low)


def pack_kernel(own, x_first, x_second, taps, first, second, read, table):
    even_x, even_y = is_even("gx"), is_even("gy")
    for f in range(3):
        read[f, HALO : HALO + NX] = own[f]
        read[f, 0:HALO] = jnp.where(even_x, x_first[f], x_second[f])
        read[f, HALO + NX :] = jnp.where(even_x, x_second[f], x_first[f])
        quarters = [pl.ds(QUARTER * q, QUARTER) for q in range(4)]
        low = jnp.concatenate([read[f, r, 0:HALO] for r in quarters], axis=1)
        high = jnp.concatenate([read[f, r, NY - HALO : NY] for r in quarters], axis=1)
        first[QUARTER * f : QUARTER * (f + 1), :] = jnp.where(even_y, low, high)
        second[QUARTER * f : QUARTER * (f + 1), :] = jnp.where(even_y, high, low)
    table[...] = jnp.zeros_like(table)
    table[0:TAPS, :] = taps[...]
    groups = [pl.ds(8 * g, 8) for g in range(TAP_ROWS // 8)]
    spare = jnp.zeros((8, 128 - 2 * TAP_ROWS), F32)
    low = jnp.concatenate([table[r, 0:HALF] for r in groups] + [spare], axis=1)
    high = jnp.concatenate([table[r, NY - HALF : NY] for r in groups] + [spare], axis=1)
    first[3 * QUARTER :, :] = jnp.where(even_y, low, high)
    second[3 * QUARTER :, :] = jnp.where(even_y, high, low)


def pack(own, x_first, x_second, taps):
    edge = jax.ShapeDtypeStruct((3 * QUARTER + 8, 128), F32)
    return pl.pallas_call(
        pack_kernel,
        out_shape=[edge, edge, jax.ShapeDtypeStruct((3, NX_READ, NY), F32)],
        in_specs=[VMEM] * 4,
        out_specs=[VMEM] * 3,
        scratch_shapes=[pltpu.VMEM((TAP_ROWS, NY), F32)],
        compiler_params=pltpu.CompilerParams(vmem_limit_bytes=8 << 20),
        cost_estimate=cost(5),
    )(own, x_first, x_second, taps)


def norm_y(taps, cell, total_cells):
    tap = lax.broadcasted_iota(jnp.int32, taps.shape, 0)
    source = cell + tap - HALF
    masked = jnp.where((source >= 0) & (source < total_cells) & (tap < TAPS), taps, 0.0)
    total = jnp.sum(masked, axis=0, keepdims=True)
    weights = masked / jnp.where(total > 0, total, 1.0)
    high = weights.astype(BF).astype(F32)
    return high, weights - high


def slanted(part, rows, cells):
    x = jnp.concatenate([part, jnp.zeros((rows - part.shape[0], 128), F32)], axis=0)
    lane = lax.broadcasted_iota(jnp.int32, x.shape, 1)
    step = 1
    while step < cells:
        x = jnp.where((lane & step) != 0, pltpu.roll(x, step, 0), x)
        step *= 2
    return x


def rolled(part, offset, lanes):
    m = part.shape[0]
    wide = jnp.concatenate([part, jnp.zeros((m, lanes - 128), F32)], axis=1)
    return pltpu.roll(wide, offset % lanes, 1, stride=1, stride_axis=0)


def y_matrix(taps_ref, first_cell, total_cells, table, out):
    table[...] = jnp.zeros_like(table)
    table[0:TAPS, :] = taps_ref[...]
    out[...] = jnp.zeros_like(out)
    for s in (0, 128):
        cell = first_cell + s + lax.broadcasted_iota(jnp.int32, (TAP_ROWS, 128), 1)
        weights = norm_y(table[:, s : s + 128], cell, total_cells)
        hi, lo = (slanted(part, 128 + 2 * HALF, 128).astype(BF) for part in weights)
        own = slice(HALF, 128 + 2 * HALF) if s == 0 else slice(0, 128 + HALF)
        halo = slice(0, HALF) if s == 0 else slice(128 + HALF, 128 + 2 * HALF)
        row = 0 if s == 0 else 128 - HALF
        halo_row = 128 - HALF if s == 0 else 0
        lanes = slice(s, s + 128)
        for base, part in ((0, hi), (NY, hi), (2 * NY, lo)):
            out[base + row : base + row + 128 + HALF, lanes] = part[own]
        for base, part in ((halo_row, hi), ((halo_row + 64) % 128, hi), (128 + halo_row, lo)):
            out[3 * NY + base : 3 * NY + base + HALF, lanes] = part[halo]


def outer_matrix(higher, lower, first_cell, total_cells, out):
    lane = lax.broadcasted_iota(jnp.int32, (TAP_ROWS, 128), 1)
    groups = [slice(HALF * g, HALF * (g + 1)) for g in range(TAP_ROWS // 8)]
    spare = jnp.zeros((8, 128 - 2 * HALF), F32)
    taps = [jnp.concatenate([higher[:, g], spare, lower[:, g]], axis=1) for g in groups]
    cell = first_cell + jnp.where(lane < 64, NY + lane, lane - 128)
    weights = norm_y(jnp.concatenate(taps, axis=0), cell, total_cells)
    hi, lo = (slanted(part, 3 * HALF, HALF) for part in weights)
    low_side = lax.broadcasted_iota(jnp.int32, hi.shape, 1) >= 64
    out[...] = jnp.zeros_like(out)
    ends = []
    for part in (hi, lo):
        high_end = jnp.where(low_side, 0.0, part).astype(BF)
        low_end = jnp.where(low_side, part, 0.0).astype(BF)
        ends.append((high_end[HALF:], low_end[0:HALO], high_end[0:HALF], low_end[HALO:]))
    for base, part in ((0, 0), (64, 0), (128, 1)):
        out[base : base + HALO, :] = ends[part][0]
    for base, part in ((96, 0), (32, 0), (128 + 96, 1)):
        out[base : base + HALO, :] = ends[part][1]
    for base, part in ((112, 0), (16, 0), (48, 1)):
        out[256 + base : 256 + base + HALF, :] = ends[part][2]
    for base, part in ((0, 0), (32, 0), (64, 1)):
        out[256 + base : 256 + base + HALF, :] = ends[part][3]


def halo_lanes(hi, lo):
    lane = lax.broadcasted_iota(jnp.int32, hi.shape, 1)
    outer = (lane < HALO) | (lane >= 128 - HALO)
    return jnp.where(outer, hi, pltpu.roll(lo.astype(F32), 64, 1).astype(BF))


def packed(tiles):
    total = tiles[0]
    for q, tile in enumerate(tiles[1:], 1):
        total = total + pltpu.roll(tile, HALO * q, 1)
    return total


def unpacked(tile, count):
    hi, lo = (part.astype(F32) for part in split(tile))
    lane = lax.broadcasted_iota(jnp.int32, tile.shape, 1)
    outer = (lane < HALO) | (lane >= 128 - HALO)
    factors = []
    for q in range(count):
        high = pltpu.roll(hi, 128 - HALO * q, 1) if q else hi
        low = pltpu.roll(lo, (64 - HALO * q) % 128, 1) if q != 2 else lo
        factors.append(jnp.concatenate([jnp.where(outer, high, low), high], axis=1).astype(BF))
    return factors


def times(left, matrix):
    return jnp.dot(left, matrix, preferred_element_type=F32)


def x_taps(taps_ref, rows):
    lane = lax.broadcasted_iota(jnp.int32, (rows, 128), 1)
    taps = jnp.zeros((rows, 128), F32)
    for t in range(TAPS):
        taps = jnp.where(lane == t, taps_ref[t], taps)
    return taps / jnp.sum(taps, axis=1, keepdims=True)


def x_matrix(taps_ref, m):
    k = m + 2 * HALF
    lanes = -(-3 * k // 128) * 128
    taps = x_taps(taps_ref, m)
    high = taps.astype(BF).astype(F32)
    low = taps - high
    total = rolled(high, 0, lanes) + rolled(high, k, lanes) + rolled(low, 2 * k, lanes)
    return total.astype(BF)


def filter_x(matrix, x, start, m):
    k = m + 2 * HALF
    hi, lo = split(x[start : start + k])
    spare = matrix.shape[1] - 3 * k
    parts = [hi, lo, hi]
    if spare:
        parts.append(jnp.zeros((spare, x.shape[1]), BF))
    return jnp.dot(matrix[...], jnp.concatenate(parts, axis=0), preferred_element_type=F32)


def matrix_kernel(grid_x, test_x, grid_y, test_y, y_grid, y_test, *rest):
    first_cell = lax.axis_index("gy") * NY
    total_cells = lax.axis_size("gy") * NY
    table = rest[-1]
    for out, (taps, m) in zip(rest[:-1], X_PARTS):
        out[...] = x_matrix((grid_x, test_x)[taps], m)
    y_matrix(grid_y, first_cell, total_cells, table, y_grid)
    y_matrix(test_y, first_cell, total_cells, table, y_test)


X_PARTS = [(0, 128), (0, 96), (0, 64), (1, 128), (1, 64)]


def matrices(grid_x, test_x, grid_y, test_y):
    return pl.pallas_call(
        matrix_kernel,
        out_shape=[
            jax.ShapeDtypeStruct((4 * NY, NY), BF),
            jax.ShapeDtypeStruct((4 * NY, NY), BF),
        ]
        + [jax.ShapeDtypeStruct((m, -(-3 * (m + 2 * HALF) // 128) * 128), BF) for _, m in X_PARTS],
        in_specs=[SMEM, SMEM, VMEM, VMEM],
        out_specs=[VMEM] * (2 + len(X_PARTS)),
        scratch_shapes=[pltpu.VMEM((TAP_ROWS, NY), F32)],
        compiler_params=pltpu.CompilerParams(vmem_limit_bytes=61 << 20),
        cost_estimate=cost(2),
    )(grid_x, test_x, grid_y, test_y)


VELOCITY_TILES = ((0, 128), (128, 128), (256, 96))
INNER_TILES = ((0, 128), (128, 128), (256, 64))


STARTS = [NX_COARSE * f for f in range(3)] + [3 * NX_COARSE + NX * p for p in range(6)]
STACK = 3 * NX_COARSE + 6 * NX


def own_kernel(read, x128, x96, x64, y_grid, part, near, hi, lo):
    x_grid = {128: x128, 96: x96, 64: x64}
    for f in range(9):
        if f < 3:
            field, tiles = read[f], VELOCITY_TILES
        else:
            i, j = PAIRS[f - 3]
            inner = slice(HALF, HALF + NX_COARSE)
            field, tiles = read[i, inner] * read[j, inner], INNER_TILES
        for start, m in tiles:
            rows = slice(STARTS[f] + start, STARTS[f] + start + m)
            hi[rows], lo[rows] = split(filter_x(x_grid[m], field, start, m))
        rows = slice(STARTS[f], STARTS[f] + (NX_COARSE if f < 3 else NX))
        if f < 3:
            near[f] = near_lanes(hi[rows], lo[rows])
    part[...] = times(jnp.concatenate([hi[...], lo[...], hi[...]], axis=1), y_grid[0 : 3 * NY])


def near_lanes(hi, lo):
    lane = lax.broadcasted_iota(jnp.int32, (hi.shape[0], 128), 1)
    ends = [jnp.where(lane < HALF, x[:, 0:128], x[:, 128:NY]).astype(F32) for x in (hi, lo)]
    low, again = pltpu.roll(ends[1], 32, 1), pltpu.roll(ends[0], 64, 1)
    ends = jnp.where((lane < HALF) | (lane >= 128 - HALF), ends[0], jnp.where(lane < 48, low, again))
    return ends.astype(BF)


def filter_own(read, x_grid, y_grid):
    return pl.pallas_call(
        own_kernel,
        out_shape=[
            jax.ShapeDtypeStruct((STACK, NY), F32),
            jax.ShapeDtypeStruct((3, NX_COARSE, 128), BF),
        ],
        in_specs=[VMEM] * 5,
        out_specs=[VMEM] * 2,
        scratch_shapes=[pltpu.VMEM((STACK, NY), BF), pltpu.VMEM((STACK, NY), BF)],
        compiler_params=pltpu.CompilerParams(vmem_limit_bytes=12 << 20),
        cost_estimate=cost(3),
    )(read, *x_grid, y_grid)


def main_kernel(
    part, ends, y_first, y_second, y_grid, y_test, x128, x96, x64, t128, t64, subgrid, germano,
    edge, smooth, coarse, tested, y_outer, buf_s, buf_g, own_hi, own_lo, halo, sems,
):
    even = is_even("gy")
    x_grid = {128: x128, 96: x96, 64: x64}
    x_test = {128: t128, 64: t64}

    def from_neighbours(rows):
        one, two = y_first[rows, :], y_second[rows, :]
        return jnp.where(even, two, one), jnp.where(even, one, two)

    higher, lower = from_neighbours(slice(3 * QUARTER, 3 * QUARTER + 8))
    cells = lax.axis_index("gy") * NY, lax.axis_size("gy") * NY
    outer_matrix(higher, lower, *cells, y_outer)
    copies = []

    def send(buffer, out, p, sem):
        copy = pltpu.make_async_copy(buffer.at[p], out.at[p], sem)
        copy.start()
        copies.append(copy)

    for f in range(3):
        higher, lower = from_neighbours(slice(QUARTER * f, QUARTER * (f + 1)))
        for q in range(4):
            lanes = slice(HALO * q, HALO * (q + 1))
            edge[QUARTER * q : QUARTER * (q + 1), 128 * f : 128 * (f + 1)] = jnp.concatenate(
                [higher[:, lanes], jnp.zeros((QUARTER, 64), F32), lower[:, lanes]], axis=1
            )
    for start, m in VELOCITY_TILES:
        smooth[start : start + m, 0:384] = filter_x(x_grid[m], edge, start, m)
    lane = lax.broadcasted_iota(jnp.int32, (NX_COARSE, 128), 1)
    near = (lane < HALF) | (lane >= 128 - HALF)
    fields = [edge[HALF : HALF + NX_COARSE, 128 * f : 128 * (f + 1)] for f in range(3)]
    fields = [jnp.where(near, field, 0.0) for field in fields]
    products = [fields[i] * fields[j] for i, j in PAIRS]
    products = jnp.concatenate([packed(products[0:4]), packed(products[4:6])], axis=1)
    for start, m in INNER_TILES:
        smooth[start : start + m, 384:] = filter_x(x_grid[m], products, start, m)

    def halo_factor(f, rows):
        hi, lo = split(smooth[0:rows, 128 * f : 128 * (f + 1)])
        return jnp.concatenate([halo_lanes(hi, lo), hi], axis=1)

    for f in range(3):
        left = halo_factor(f, NX_COARSE)
        coarse[f, :, 0:NY] = part[STARTS[f] : STARTS[f] + NX_COARSE] + times(left, y_grid[3 * NY :])
        coarse[f, :, NY:] = times(jnp.concatenate([left, ends[f]], axis=1), y_outer[...])
    own = slice(HALF, HALF + NX)
    factors = unpacked(smooth[0:NX, 384:512], 4) + unpacked(smooth[0:NX, 512:640], 2)
    for p, (i, j) in enumerate(PAIRS):
        rows = slice(STARTS[3 + p], STARTS[3 + p] + NX)
        stress = part[rows] + times(factors[p], y_grid[3 * NY :])
        buf_s[p] = stress - coarse[i, own, 0:NY] * coarse[j, own, 0:NY]
        send(buf_s, subgrid, p, sems.at[p])
    def test_field(f, lanes):
        if f < 3:
            return coarse[f, :, lanes]
        i, j = PAIRS[f - 3]
        return coarse[i, :, lanes] * coarse[j, :, lanes]

    groups = [range(0, 4), range(4, 8), range(8, 9)]
    halos = [packed([test_field(f, slice(NY, RING)) for f in group]) for group in groups]
    halos = jnp.concatenate(halos, axis=1)
    for start, m in INNER_TILES:
        smooth[start : start + m, 0:384] = filter_x(x_test[m], halos, start, m)
    for n, group in enumerate(groups):
        for f, factor in zip(group, unpacked(smooth[0:NX, 128 * n : 128 * (n + 1)], len(group))):
            halo[NX * f : NX * (f + 1)] = factor
    for first, last in ((0, 3), (3, 6), (6, 8), (8, 9)):
        for f in range(first, last):
            field = test_field(f, slice(0, NY))
            for start, m in INNER_TILES:
                rows = slice(NX * f + start, NX * f + start + m)
                own_hi[rows], own_lo[rows] = split(filter_x(x_test[m], field, start, m))
        rows = slice(NX * first, NX * last)
        left = jnp.concatenate([own_hi[rows], own_lo[rows], own_hi[rows], halo[rows]], axis=1)
        results = times(left, y_test[...])
        for f in range(first, last):
            result = results[NX * (f - first) : NX * (f - first + 1)]
            if f < 3:
                tested[f] = result
            else:
                i, j = PAIRS[f - 3]
                buf_g[f - 3] = result - tested[i] * tested[j]
                send(buf_g, germano, f - 3, sems.at[3 + f])
    for copy in copies:
        copy.wait()


def main(part, near, y_first, y_second, y_grid, y_test, x_parts):
    out = jax.ShapeDtypeStruct((6, NX, NY), F32)
    return pl.pallas_call(
        main_kernel,
        out_shape=[out, out],
        in_specs=[VMEM] * (6 + len(x_parts)),
        out_specs=[HBM, HBM],
        scratch_shapes=[
            pltpu.VMEM((NX_READ, 3 * 128), F32),
            pltpu.VMEM((NX_COARSE, 5 * 128), F32),
            pltpu.VMEM((3, NX_COARSE, RING), F32),
            pltpu.VMEM((3, NX, NY), F32),
            pltpu.VMEM((3 * 128, 128), BF),
            pltpu.VMEM((6, NX, NY), F32),
            pltpu.VMEM((6, NX, NY), F32),
            pltpu.VMEM((9 * NX, NY), BF),
            pltpu.VMEM((9 * NX, NY), BF),
            pltpu.VMEM((9 * NX, NY), BF),
            pltpu.SemaphoreType.DMA((12,)),
        ],
        compiler_params=pltpu.CompilerParams(vmem_limit_bytes=24 << 20),
    )(part, near, y_first, y_second, y_grid, y_test, *x_parts)


def swaps(axis, first, periodic):
    count = lax.axis_size(axis)
    last = count if periodic else count - 1
    pairs = [(i, (i + 1) % count) for i in range(first, last, 2)]
    return pairs + [(b, a) for a, b in pairs]


def local(velocity, grid_x, grid_y, test_x, test_y):
    velocity = velocity.reshape(3, NY, NX).swapaxes(1, 2)
    first, second = edges(velocity)
    x_first = lax.ppermute(first, "gx", swaps("gx", 1, True))
    x_second = lax.ppermute(second, "gx", swaps("gx", 0, True))
    y_grid, y_test, *x_parts = matrices(grid_x, test_x, grid_y.T, test_y.T)
    first, second, read = pack(velocity, x_first, x_second, grid_y.T)
    y_first = lax.ppermute(first, "gy", swaps("gy", 1, False))
    y_second = lax.ppermute(second, "gy", swaps("gy", 0, False))
    part, near = filter_own(read, x_parts[:3], y_grid)
    outs = main(part, near, y_first, y_second, y_grid, y_test, x_parts)
    return tuple(out.swapaxes(1, 2).reshape(6, 1, NY, NX) for out in outs)


def solution(mesh):
    placed = (P(None, None, "gy", "gx"), P(), P("gy", None), P(), P("gy", None))
    return jax.shard_map(
        local,
        mesh=mesh,
        in_specs=placed,
        out_specs=(P(None, None, "gy", "gx"), P(None, None, "gy", "gx")),
        check_vma=False,
    )
```
